256 devices in a mesh: wide: 32 (over z, x), narrow: 8 (over y, core).
Axes of the slice: x: 4, y: 4, z: 8, core: 2. Of those that a mesh axis runs over, the one named last changes fastest.
Arguments:
- tokens: bfloat16 [32, 9216, 1280], P('wide', 'narrow'), may hold values from -64 to 64
- slot_keys: bfloat16 [1280, 256], P(None, 'wide'), may hold values from -2 to 2
- w_in: bfloat16 [64, 1280, 5120], P('wide', None, 'narrow'), may hold values from -0.15625 to 0.15625
- b_in: bfloat16 [64, 5120], P('wide', 'narrow'), may hold values from -3 to 3
- w_out: bfloat16 [64, 5120, 1280], P('wide', 'narrow'), may hold values from -0.078125 to 0.078125
- b_out: bfloat16 [64, 1280], P('wide'), may hold values from -1.1953125 to 1.1953125
Outputs:
- mixed_out: bfloat16 [32, 9216, 1280], P('wide', 'narrow')
The draws below stay inside these ranges and needn't reach their ends.
All inputs are finite; a program needn't handle non-finite values.
Results may differ from the reference program's by a relative error of at most 0.0064.
Values may be sent and summed in bfloat16 or wider, within the bound.
A program may use at most 64 MiB of HBM per device.

```python
import math
from functools import partial
import jax
import jax.numpy as jnp
from jax import lax

D = 1280
FF = 5120
SLOTS_PER = 4
EXPERTS = 64
SLOTS = 256
LEN = 9216
CLIPS = 32


def slot_key_columns(key):
    key_base, key_scale = jax.random.split(key)
    base = jnp.clip(jax.random.normal(key_base, (D, SLOTS), jnp.float32), -4.0, 4.0) * (1.5 / math.sqrt(D))
    col_scale = jnp.exp(jax.random.uniform(key_scale, (1, SLOTS), jnp.float32, math.log(0.7), math.log(1.4)))
    columns = base * col_scale
    for pair in range(3):
        first_slot = (37 * pair + 1) % SLOTS
        second_slot = (37 * pair + 20) % SLOTS
        col_first = columns[:, first_slot]
        col_first = col_first * (3.0 / jnp.sqrt(jnp.sum(col_first * col_first)))
        col_second = columns[:, second_slot]
        col_second = col_second - jnp.sum(col_second * col_first) / 9.0 * col_first
        col_second = col_second * (3.0 / jnp.sqrt(jnp.sum(col_second * col_second)))
        columns = columns.at[:, first_slot].set(columns[:, first_slot])
        columns = columns.at[:, second_slot].set(columns[:, second_slot])
    return jnp.clip(columns, -2.0, 2.0)


def draw_slot_keys(key, part):
    columns = slot_key_columns(key)
    return columns.astype(jnp.bfloat16)


def draw_tokens(key, part):
    key = jax.random.fold_in(key, 7)
    key_noise, key_scale = jax.random.split(key, 2)
    base_noise = jnp.clip(jax.random.normal(key_noise, (CLIPS, LEN, D), jnp.float32), -4.0, 4.0)
    row_scale = jnp.exp(jax.random.uniform(key_scale, (CLIPS, LEN, 1), jnp.float32, math.log(0.5), math.log(2.0)))
    values = row_scale * base_noise
    return jnp.clip(values, -64.0, 64.0).astype(jnp.bfloat16)


def block_levels(key, shape, cuts, smallest, largest):
    factor_of, own = 1.0, jax.random.fold_in(key, 6)
    for position, shards_of in cuts:
        steps = jnp.exp(jax.random.uniform(jax.random.fold_in(own, position), (shards_of,), jnp.float32, smallest / len(cuts), largest / len(cuts)))
        factor_of = factor_of * jnp.repeat(steps, shape[position] // shards_of).reshape([-1 if axis == position else 1 for axis in range(len(shape))])
    return factor_of


def noise(rng, dims, deviation, most, cuts=(), dtype=jnp.bfloat16):
    loudness = block_levels(rng, dims, cuts, -0.22, 0.18) if cuts else 1.0
    array = jax.random.normal(rng, dims, jnp.float32) * deviation * loudness
    return jnp.minimum(jnp.maximum(array, -most), most).astype(dtype)


def setup_inputs(seed: int = 0) -> dict:
    keys = jax.random.split(jax.random.key(seed), 7)
    return {
        "tokens": draw_tokens(jax.random.fold_in(keys[6], 71), 0),
        "slot_keys": draw_slot_keys(jax.random.fold_in(keys[6], 71), 0),
        "w_in": noise(keys[2], (EXPERTS, D, FF), D ** -0.5, 0.15625, ((0, 32), (2, 8))),
        "b_in": noise(keys[3], (EXPERTS, FF), 0.5, 3.0, ((0, 32), (1, 8))),
        "w_out": noise(keys[4], (EXPERTS, FF, D), FF ** -0.5, 0.078125, ((0, 32), (1, 8))),
        "b_out": noise(keys[5], (EXPERTS, D), 0.2, 1.1953125, ((0, 32),)),
    }


def clip_slots(slot_keys, clip_tokens):
    logits = jnp.dot(clip_tokens, slot_keys, preferred_element_type=jnp.float32)
    spread = jnp.exp(logits - jnp.max(logits, axis=0, keepdims=True))
    totals = jnp.sum(spread, axis=0)
    dispatch = spread.astype(jnp.bfloat16)
    slot_sums = jnp.dot(dispatch.T, clip_tokens, preferred_element_type=jnp.float32)
    return (slot_sums / totals[:, None]).astype(jnp.bfloat16)


def expert_apply(items):
    slot_rows, w_first, b_first, w_second, b_second = items
    hidden = jnp.einsum("csd,df->csf", slot_rows.astype(jnp.float32), w_first.astype(jnp.float32))
    hidden = jax.nn.gelu(hidden + b_first.astype(jnp.float32), approximate=True).astype(jnp.bfloat16)
    result = jnp.einsum("csf,fd->csd", hidden.astype(jnp.float32), w_second.astype(jnp.float32))
    return (result + b_second.astype(jnp.float32)).astype(jnp.bfloat16)


def clip_combine(slot_keys, items):
    clip_tokens, clip_outputs = items
    logits = jnp.dot(clip_tokens, slot_keys, preferred_element_type=jnp.float32)
    row_spread = jnp.exp(logits - jnp.max(logits, axis=1, keepdims=True))
    row_totals = jnp.sum(row_spread, axis=1, keepdims=True)
    combine = row_spread.astype(jnp.bfloat16)
    summed = jnp.dot(combine, clip_outputs, preferred_element_type=jnp.float32)
    return (summed / row_totals).astype(jnp.bfloat16)


def reference(tokens, slot_keys, w_in, b_in, w_out, b_out):
    slot_inputs = lax.map(partial(clip_slots, slot_keys), tokens)
    grouped = slot_inputs.reshape(CLIPS, EXPERTS, SLOTS_PER, D).transpose(1, 0, 2, 3)
    expert_out = lax.map(expert_apply, (grouped, w_in, b_in[:, None, None, :], w_out, b_out[:, None, None, :]))
    expert_out = expert_out.transpose(1, 0, 2, 3).reshape(CLIPS, SLOTS, D)
    return lax.map(partial(clip_combine, slot_keys), (tokens, expert_out))
```

```python
import jax
import jax.numpy as jnp
from jax import lax
from jax.experimental import pallas as pl
from jax.experimental.pallas import tpu as pltpu
from jax.sharding import PartitionSpec as P

MESH = pl.DeviceIdType.MESH
BF = jnp.bfloat16
F32 = jnp.float32
NZ, NX, NY = 8, 4, 4
OWN = 8
D = 1280


def kernel(
    tok_hbm, key_hbm, win_hbm, bin_ref, wout_hbm, bout_ref,
    comb_ref, back_ref,
    tok, win, wout, own_key, keys, lt, comb,
    sums, stat, sib_sums, sib_stat, half, half_stat, far, far_stat,
    ready, slots_in, part, sib_part, half2, far2, ready2, back,
    load_sem, key_send, key_recv, fwd_send, fwd_recv,
    a_send, a_recv, b_send, b_recv, c_send, c_recv, d_send, d_recv, e_send, e_recv,
    f_send, f_recv, g_send, g_recv, i_send, i_recv, j_send, j_recv, k_send, k_recv,
):
    w, n = lax.axis_index("wide"), lax.axis_index("narrow")
    z, x = w // NX, lax.rem(w, NX)
    y, c = n // 2, lax.rem(n, 2)
    sib = (w, y * 2 + 1 - c)
    h = lax.rem(z // 4 + c, 2)
    gx = lax.rem(y + NX - x, NX)

    def y_peer(k):
        return (w, lax.rem(y + k, NY) * 2 + c)

    def send(src, dst, s_sem, r_sem, dev):
        cp = pltpu.make_async_remote_copy(
            src_ref=src, dst_ref=dst, send_sem=s_sem, recv_sem=r_sem, device_id=dev, device_id_type=MESH
        )
        cp.start()
        return cp

    def wait_for(ref, sem):
        pltpu.make_async_copy(ref, ref, sem).wait()

    loads = [
        pltpu.make_async_copy(key_hbm, own_key, load_sem.at[0]),
        pltpu.make_async_copy(tok_hbm, tok, load_sem.at[1]),
        pltpu.make_async_copy(win_hbm, win, load_sem.at[2]),
        pltpu.make_async_copy(wout_hbm, wout, load_sem.at[3]),
    ]
    for cp in loads:
        cp.start()

    barrier = pltpu.get_barrier_semaphore()

    def greet(w_to, n_to):
        pl.semaphore_signal(barrier, inc=1, device_id=(w_to, n_to), device_id_type=MESH)

    greet(*sib)
    for k in range(1, NY):
        greet(*y_peer(k))
    order = (4, 3, 5, 2, 6, 1, 7, 0)

    def key_peer(di, dz):
        return (lax.rem(z + dz, NZ) * NX + lax.rem(x + c + 2 * di, NX), n)

    for dz in order:
        for di in (1, 0):
            if di == 0 and dz == 0:
                @pl.when(c == 1)
                def _():
                    greet(*key_peer(0, 0))
            else:
                greet(*key_peer(di, dz))
    pl.semaphore_wait(barrier, 1 + (NY - 1) + 2 * NZ - 1 + c)
    loads[0].wait()

    own_copy = pltpu.make_async_copy(own_key, keys.at[x, z], key_recv.at[0])
    key_copies = []
    for i, dz in enumerate(order):
        for di in (1, 0):
            cp = pltpu.make_async_remote_copy(
                src_ref=own_key, dst_ref=keys.at[x, z], send_sem=key_send.at[di * NZ + dz],
                recv_sem=key_recv.at[di], device_id=key_peer(di, dz), device_id_type=MESH,
            )
            if di == 0 and dz == 0:
                @pl.when(c == 1)
                def _():
                    cp.start()
                @pl.when(c == 0)
                def _():
                    own_copy.start()
            else:
                cp.start()
            key_copies.append((di, dz, cp))
    fwd = []
    for di in (0, 1):
        xs = lax.rem(x + NX - c - 2 * di + NX, NX)
        wait_for(keys.at[xs], key_recv.at[di])
        fwd.append(send(keys.at[xs], keys.at[xs], fwd_send.at[di], fwd_recv.at[di], sib))
    for di in (0, 1):
        xs = lax.rem(x + NX - (1 - c) - 2 * di + NX, NX)
        wait_for(keys.at[xs], fwd_recv.at[di])
    loads[1].wait()

    key_rows = keys[...].reshape(NX * NZ * OWN, D)
    tokens = tok.shape[0]
    step = tokens // 3
    for i in range(3):
        lt[:, i * step:(i + 1) * step] = lax.dot_general(
            key_rows, tok[i * step:(i + 1) * step, :], (((1,), (1,)), ((), ())), preferred_element_type=F32
        )
    logits_t = lt[...]
    top = jnp.max(logits_t, axis=1, keepdims=True)
    spread = jnp.exp(logits_t - top)
    totals = jnp.sum(spread, axis=1, keepdims=True)
    dispatch = spread.astype(BF)
    slots = dispatch.shape[0]
    lane = lax.broadcasted_iota(jnp.int32, (slots, 128), 1)
    stat[...] = jnp.where(lane < 64, top, totals).reshape(stat.shape)
    for i in range(5):
        cols = slice(i * 256, (i + 1) * 256)
        sums[:, :, :, cols] = (
            jnp.dot(dispatch, tok[:, cols], preferred_element_type=F32).astype(BF).reshape(NX, 2, 32, 256)
        )

    a = [
        send(sums.at[:, 1 - h], sib_sums, a_send.at[0], a_recv.at[0], sib),
        send(stat.at[:, 1 - h], sib_stat, a_send.at[1], a_recv.at[1], sib),
    ]

    for i in range(4):
        rows = slice(i * (tokens // 4), (i + 1) * (tokens // 4))
        logits = lax.dot_general(
            tok[rows, :], key_rows, (((1,), (1,)), ((), ())), preferred_element_type=F32
        )
        row_spread = jnp.exp(logits - jnp.max(logits, axis=1, keepdims=True))
        comb[rows, :] = (row_spread / jnp.sum(row_spread, axis=1, keepdims=True)).astype(BF)
    comb_out = pltpu.make_async_copy(comb, comb_ref, load_sem.at[4])
    comb_out.start()

    for cp in a:
        cp.wait_recv()
    lane = lax.broadcasted_iota(jnp.int32, (32, 128), 1)
    for j in range(NX):
        st_a, st_b = stat[j, h], sib_stat[j]
        m_a, t_a, m_b, t_b = st_a[:, 0:1], st_a[:, 64:65], st_b[:, 0:1], st_b[:, 64:65]
        m = jnp.maximum(m_a, m_b)
        f_a, f_b = jnp.exp(m_a - m), jnp.exp(m_b - m)
        half[j] = (sums[j, h].astype(F32) * f_a + sib_sums[j].astype(F32) * f_b).astype(BF)
        half_stat[j] = jnp.where(lane < 64, m, t_a * f_a + t_b * f_b)

    b = []
    for k in (2, 1, 3):
        to = lax.rem(y + k + NX - x, NX)
        b.append(send(half.at[to], far.at[k - 1], b_send.at[k - 1], b_recv.at[k - 1], y_peer(k)))
        b.append(send(half_stat.at[to], far_stat.at[k - 1], b_send.at[k + 2], b_recv.at[k + 2], y_peer(k)))
    for cp in b:
        cp.wait_recv()
    st = [half_stat[gx]] + [far_stat[k] for k in range(3)]
    ms = [s[:, 0:1] for s in st]
    ts = [s[:, 64:65] for s in st]
    m = jnp.maximum(jnp.maximum(ms[0], ms[1]), jnp.maximum(ms[2], ms[3]))
    fs = [jnp.exp(mi - m) for mi in ms]
    inv = 1.0 / (ts[0] * fs[0] + ts[1] * fs[1] + ts[2] * fs[2] + ts[3] * fs[3])
    acc = half[gx].astype(F32) * (fs[0] * inv)
    for k in range(3):
        acc = acc + far[k].astype(F32) * (fs[k + 1] * inv)
    ready[...] = acc.reshape(4, OWN, D).astype(BF)

    def plane(src, there, here, s_sem, r_sem):
        copies = []
        for i in range(4):
            w_to = (4 * h + i) * NX + gx
            cp = pltpu.make_async_remote_copy(
                src_ref=src.at[i], dst_ref=there, send_sem=s_sem.at[i], recv_sem=r_sem,
                device_id=(w_to, n), device_id_type=MESH,
            )

            @pl.when(w_to != w)
            def _():
                cp.start()

            @pl.when(w_to == w)
            def _():
                pltpu.make_async_copy(src.at[i], there, r_sem).start()

            copies.append((w_to, cp))
        wait_for(here, r_sem)
        return copies

    def gather(place, y_send, y_recv, s_send, s_recv):
        own = place(y, c)
        copies = [send(own, own, y_send.at[k - 1], y_recv.at[k - 1], y_peer(k)) for k in (2, 1, 3)]
        copies.append(send(own, own, s_send.at[0], s_recv.at[0], sib))
        for k in (1, 3, 2):
            got = place(lax.rem(y + NY - k, NY), c)
            wait_for(got, y_recv.at[k - 1])
            copies.append(send(got, got, s_send.at[k], s_recv.at[k], sib))
        for k in range(NY):
            wait_for(place(lax.rem(y + NY - k, NY), 1 - c), s_recv.at[k])
        return copies

    p1 = plane(ready, slots_in.at[n, lax.rem(z, 4)], slots_in.at[n], c_send, c_recv)
    g1 = gather(lambda yy, cc: slots_in.at[yy * 2 + cc], d_send, d_recv, e_send, e_recv)

    loads[2].wait()
    loads[3].wait()
    rows_in = slots_in[...].reshape(slots, D)
    first = lax.rem(lax.broadcasted_iota(jnp.int32, (slots, 1), 0), OWN) < 4
    b_in = bin_ref[...].astype(F32)
    hid = jnp.where(
        first,
        jnp.dot(rows_in, win[0], preferred_element_type=F32) + b_in[0:1],
        jnp.dot(rows_in, win[1], preferred_element_type=F32) + b_in[1:2],
    )
    hid = jax.nn.gelu(hid, approximate=True)
    hid0 = jnp.where(first, hid, 0.0).astype(BF)
    hid1 = jnp.where(first, 0.0, hid).astype(BF)
    for i in range(5):
        cols = slice(i * 256, (i + 1) * 256)
        out = jnp.dot(hid0, wout[0, :, cols], preferred_element_type=F32)
        out = out + jnp.dot(hid1, wout[1, :, cols], preferred_element_type=F32)
        part[:, :, :, cols] = out.astype(BF).reshape(NY, 2, 32, 256)

    f = send(part.at[:, 1 - c], sib_part, f_send, f_recv, sib)
    f.wait_recv()
    for j in range(NY):
        half2[j] = (part[j, c].astype(F32) + sib_part[j].astype(F32)).astype(BF)
    gs = [send(half2.at[lax.rem(y + k, NY)], far2.at[k - 1], g_send.at[k - 1], g_recv.at[k - 1], y_peer(k)) for k in (2, 1, 3)]
    for cp in gs:
        cp.wait_recv()
    b_out = bout_ref[...].astype(F32)
    first32 = lax.rem(lax.broadcasted_iota(jnp.int32, (32, 1), 0), OWN) < 4
    acc = half2[y].astype(F32) + jnp.where(first32, b_out[0:1], b_out[1:2])
    for k in range(3):
        acc = acc + far2[k].astype(F32)
    ready2[...] = acc.reshape(4, OWN, D).astype(BF)

    p2 = plane(ready2, back.at[x, z // 4, lax.rem(z, 4)], back.at[gx, h], i_send, i_recv)
    g2 = gather(
        lambda yy, cc: back.at[lax.rem(yy + NX - x, NX), lax.rem(z // 4 + cc, 2)], j_send, j_recv, k_send, k_recv
    )
    out_copy = pltpu.make_async_copy(back, back_ref, load_sem.at[5])
    out_copy.start()

    for di, dz, cp in key_copies:
        if di == 0 and dz == 0:
            @pl.when(c == 1)
            def _():
                cp.wait_send()
        else:
            cp.wait_send()
    for cp in fwd + a + b + g1 + [f] + gs + g2:
        cp.wait_send()
    for w_to, cp in p1 + p2:
        @pl.when(w_to != w)
        def _():
            cp.wait_send()
    comb_out.wait()
    out_copy.wait()


def on_device(tokens, slot_keys, w_in, b_in, w_out, b_out):
    rows = tokens.shape[1]
    slots = NZ * NX * OWN
    hbm = pl.BlockSpec(memory_space=pl.ANY)
    vmem = pl.BlockSpec(memory_space=pltpu.VMEM)
    dma = pltpu.SemaphoreType.DMA
    block = (4, OWN, D)
    comb, back = pl.pallas_call(
        kernel,
        out_shape=(
            jax.ShapeDtypeStruct((rows, slots), BF),
            jax.ShapeDtypeStruct((NX, 2) + block, BF),
        ),
        in_specs=[hbm, hbm, hbm, vmem, hbm, vmem],
        out_specs=(hbm, hbm),
        scratch_shapes=[
            pltpu.VMEM((rows, D), BF),
            pltpu.VMEM(w_in.shape, BF),
            pltpu.VMEM(w_out.shape, BF),
            pltpu.VMEM((OWN, D), BF),
            pltpu.VMEM((NX, NZ, OWN, D), BF),
            pltpu.VMEM((slots, rows), F32),
            pltpu.VMEM((rows, slots), BF),
            pltpu.VMEM((NX, 2, 32, D), BF),
            pltpu.VMEM((NX, 2, 32, 128), F32),
            pltpu.VMEM((NX, 32, D), BF),
            pltpu.VMEM((NX, 32, 128), F32),
            pltpu.VMEM((NX, 32, D), BF),
            pltpu.VMEM((NX, 32, 128), F32),
            pltpu.VMEM((3, 32, D), BF),
            pltpu.VMEM((3, 32, 128), F32),
            pltpu.VMEM(block, BF),
            pltpu.VMEM((8,) + block, BF),
            pltpu.VMEM((NY, 2, 32, D), BF),
            pltpu.VMEM((NY, 32, D), BF),
            pltpu.VMEM((NY, 32, D), BF),
            pltpu.VMEM((3, 32, D), BF),
            pltpu.VMEM(block, BF),
            pltpu.VMEM((NX, 2) + block, BF),
            dma((6,)), dma((16,)), dma((2,)), dma((2,)), dma((2,)),
            dma((2,)), dma((2,)), dma((6,)), dma((6,)), dma((4,)), dma, dma((3,)), dma((3,)), dma((4,)), dma((4,)),
            dma, dma, dma((3,)), dma((3,)), dma((4,)), dma, dma((3,)), dma((3,)), dma((4,)), dma((4,)),
        ],
        compiler_params=pltpu.CompilerParams(
            collective_id=0, has_side_effects=True, vmem_limit_bytes=48 * 1024 * 1024
        ),
    )(tokens[0], slot_keys.T, w_in, b_in, w_out, b_out)
    mixed = jnp.dot(comb, back.reshape(slots, D), preferred_element_type=F32)
    return mixed.astype(BF)[None]


def solution(mesh):
    in_specs = (
        P("wide", "narrow", None),
        P(None, "wide"),
        P("wide", None, "narrow"),
        P("wide", "narrow"),
        P("wide", "narrow", None),
        P("wide", None),
    )
    return jax.shard_map(
        on_device, mesh=mesh, in_specs=in_specs, out_specs=P("wide", "narrow", None), check_vma=False
    )
```

```python
import jax
import jax.numpy as jnp
from jax import lax
from jax.experimental import pallas as pl
from jax.experimental.pallas import tpu as pltpu
from jax.sharding import PartitionSpec as P

MESH = pl.DeviceIdType.MESH
BF = jnp.bfloat16
F32 = jnp.float32
NZ, NX, NY = 8, 4, 4
OWN = 8
D = 1280
PARTS = ((0, 768), (768, 512))
Q = len(PARTS)


def kernel(
    tok_hbm, key_hbm, win_hbm, bin_hbm, wout_hbm, bout_hbm,
    comb_ref, back,
    tok, win, wout, b_in, b_out, own_key, keys, lt, comb,
    sums, stat, sib_sums, sib_stat, own_sums, half, half_stat, far, far_stat,
    ready, slots_in, part, own_part, sib_part, half2, own2, far2, ready2,
    load_sem, key_send, key_recv, fwd_send, fwd_recv,
    as_send, as_recv, a_send, a_recv, bs_send, bs_recv, b_send, b_recv,
    c_send, c_recv, d_send, d_recv, e_send, e_recv,
    f_send, f_recv, g_send, g_recv, i_send, i_recv, j_send, j_recv, k_send, k_recv,
):
    w, n = lax.axis_index("wide"), lax.axis_index("narrow")
    z, x = w // NX, lax.rem(w, NX)
    y, c = n // 2, lax.rem(n, 2)
    sib = (w, y * 2 + 1 - c)
    h = lax.rem(z // 4 + c, 2)
    q_half = 1 - h
    gx = lax.rem(y + NX - x, NX)
    tokens = tok.shape[0]
    started = []

    def y_peer(k):
        return (w, lax.rem(y + k, NY) * 2 + c)

    def cols(q):
        return pl.ds(*PARTS[q])

    def remote(src, dst, s_sem, r_sem, dev):
        return pltpu.make_async_remote_copy(
            src_ref=src, dst_ref=dst, send_sem=s_sem, recv_sem=r_sem, device_id=dev, device_id_type=MESH
        )

    def send(src, dst, s_sem, r_sem, dev):
        cp = remote(src, dst, s_sem, r_sem, dev)
        cp.start()
        started.append((None, cp))

    def send_wide(src, dst, s_sem, r_sem, w_to):
        cp = remote(src, dst, s_sem, r_sem, (w_to, n))

        @pl.when(w_to != w)
        def _():
            cp.start()

        @pl.when(w_to == w)
        def _():
            pltpu.make_async_copy(src, dst, r_sem).start()

        started.append((w_to, cp))

    def drain():
        for w_to, cp in started:
            if w_to is None:
                cp.wait_send()
            else:
                @pl.when(w_to != w)
                def _():
                    cp.wait_send()
        started.clear()

    def wait_for(ref, sem):
        pltpu.make_async_copy(ref, ref, sem).wait()

    loads = [
        pltpu.make_async_copy(src, dst, load_sem.at[i])
        for i, (src, dst) in enumerate((
            (key_hbm, own_key), (tok_hbm, tok),
            (win_hbm.at[0], win.at[:, pl.ds(0, 640)]), (win_hbm.at[1], win.at[:, pl.ds(640, 640)]),
            (wout_hbm, wout), (bin_hbm, b_in), (bout_hbm, b_out),
        ))
    ]
    for cp in loads:
        cp.start()

    barrier = pltpu.get_barrier_semaphore()

    def greet(w_to, n_to):
        pl.semaphore_signal(barrier, inc=1, device_id=(w_to, n_to), device_id_type=MESH)

    key_peers = [(dx, (4 * q_half + i) * NX + lax.rem(x + dx, NX)) for dx in (2, 1, 3, 0) for i in range(4)]
    for dx, w_to in key_peers:
        if dx:
            greet(w_to, n)
        else:
            @pl.when(w_to != w)
            def _():
                greet(w_to, n)
    for k in (2, 1, 3):
        greet(*y_peer(k))
    greet(*sib)
    pl.semaphore_wait(barrier, 20 - c)
    loads[0].wait()

    for p, (dx, w_to) in enumerate(key_peers):
        dst = keys.at[x, z // 4, lax.rem(z, 4)]
        if dx:
            send(own_key, dst, key_send.at[p], key_recv.at[dx], (w_to, n))
        else:
            send_wide(own_key, dst, key_send.at[p], key_recv.at[dx], w_to)
    loads[1].wait()
    for dx in (0, 1, 3, 2):
        got = keys.at[lax.rem(x + NX - dx, NX), q_half]
        wait_for(got, key_recv.at[dx])
        send(got, got, fwd_send.at[dx], fwd_recv.at[dx], sib)

    def column_softmax(half_index):
        key_rows = keys[:, half_index].reshape(128, D)
        step = tokens // 3
        for i in range(3):
            lt[:, i * step:(i + 1) * step] = lax.dot_general(
                key_rows, tok[i * step:(i + 1) * step, :], (((1,), (1,)), ((), ())), preferred_element_type=F32
            )
        logits = lt[...]
        top = jnp.max(logits, axis=1, keepdims=True)
        spread = jnp.exp(logits - top)
        return top, jnp.sum(spread, axis=1, keepdims=True), spread.astype(BF)

    lane = lax.broadcasted_iota(jnp.int32, (128, 128), 1)
    top, totals, dispatch = column_softmax(q_half)
    stat[...] = jnp.where(lane < 64, top, totals).reshape(NX, 32, 128)
    send(stat, sib_stat, as_send, as_recv, sib)
    for q, (at, size) in enumerate(PARTS):
        sums[:, :, cols(q)] = (
            jnp.dot(dispatch, tok[:, cols(q)], preferred_element_type=F32).astype(BF).reshape(NX, 32, size)
        )
        send(sums.at[:, :, cols(q)], sib_sums.at[:, :, cols(q)], a_send.at[q], a_recv.at[q], sib)
    for dx in (0, 1, 3, 2):
        wait_for(keys.at[lax.rem(x + NX - dx, NX), h], fwd_recv.at[dx])
    top, totals, dispatch = column_softmax(h)
    wait_for(sib_stat, as_recv)
    other = sib_stat[...].reshape(128, 128)
    other_top, other_totals = other[:, 0:1], other[:, 64:65]
    chip_top = jnp.maximum(top, other_top)
    own_scale, other_scale = jnp.exp(top - chip_top), jnp.exp(other_top - chip_top)
    chip_totals = totals * own_scale + other_totals * other_scale
    half_stat[...] = jnp.where(lane < 64, chip_top, chip_totals).reshape(NX, 32, 128)
    for k in (2, 1, 3):
        to = lax.rem(y + k + NX - x, NX)
        send(half_stat.at[to], far_stat.at[k - 1], bs_send.at[k - 1], bs_recv.at[k - 1], y_peer(k))
    for q, (at, size) in enumerate(PARTS):
        mine = jnp.dot(dispatch, tok[:, cols(q)], preferred_element_type=F32) * own_scale
        wait_for(sib_sums.at[:, :, cols(q)], a_recv.at[q])
        chip = mine + sib_sums[:, :, cols(q)].astype(F32).reshape(128, size) * other_scale
        own_sums[:, :, cols(q)] = chip.reshape(NX, 32, size)
        half[:, :, cols(q)] = chip.astype(BF).reshape(NX, 32, size)
        for k in (2, 1, 3):
            to = lax.rem(y + k + NX - x, NX)
            send(half.at[to, :, cols(q)], far.at[k - 1, :, cols(q)], b_send.at[q, k - 1], b_recv.at[q, k - 1], y_peer(k))

    key_rows = keys[...].reshape(256, D)
    for i in range(4):
        rows = slice(i * (tokens // 4), (i + 1) * (tokens // 4))
        logits = lax.dot_general(
            tok[rows, :], key_rows, (((1,), (1,)), ((), ())), preferred_element_type=F32
        )
        row_spread = jnp.exp(logits - jnp.max(logits, axis=1, keepdims=True))
        comb[rows, :] = (row_spread / jnp.sum(row_spread, axis=1, keepdims=True)).astype(BF)
    comb_out = pltpu.make_async_copy(comb, comb_ref, load_sem.at[7])
    comb_out.start()

    for k in (1, 3, 2):
        wait_for(far_stat.at[k - 1], bs_recv.at[k - 1])
    st = [half_stat[gx]] + [far_stat[k] for k in range(3)]
    ms = [s[:, 0:1] for s in st]
    ts = [s[:, 64:65] for s in st]
    m = jnp.maximum(jnp.maximum(ms[0], ms[1]), jnp.maximum(ms[2], ms[3]))
    fs = [jnp.exp(mi - m) for mi in ms]
    inv = 1.0 / (ts[0] * fs[0] + ts[1] * fs[1] + ts[2] * fs[2] + ts[3] * fs[3])
    fs = [f * inv for f in fs]

    def plane(src, there, s_sem, r_sem):
        for i in range(4):
            send_wide(src(i), there, s_sem.at[i], r_sem, (4 * h + i) * NX + gx)

    def gather_start(place, y_send, y_recv, s_send, s_recv):
        own = place(y, c)
        for k in (2, 1, 3):
            send(own, own, y_send.at[k - 1], y_recv.at[k - 1], y_peer(k))
        send(own, own, s_send.at[0], s_recv.at[0], sib)

    def gather_forward(place, y_send, y_recv, s_send, s_recv):
        for k in (1, 3, 2):
            got = place(lax.rem(y + NY - k, NY), c)
            wait_for(got, y_recv.at[k - 1])
            send(got, got, s_send.at[k], s_recv.at[k], sib)

    def gather_end(place, y_send, y_recv, s_send, s_recv):
        for k in range(NY):
            wait_for(place(lax.rem(y + NY - k, NY), 1 - c), s_recv.at[k])

    for q, (at, size) in enumerate(PARTS):
        for k in (1, 3, 2):
            wait_for(far.at[k - 1, :, cols(q)], b_recv.at[q, k - 1])
        acc = own_sums[gx, :, cols(q)] * fs[0]
        for k in range(3):
            acc = acc + far[k, :, cols(q)].astype(F32) * fs[k + 1]
        ready[:, :, cols(q)] = acc.reshape(4, OWN, size).astype(BF)
        plane(
            lambda i: ready.at[i, :, cols(q)], slots_in.at[n, lax.rem(z, 4), :, cols(q)], c_send.at[q], c_recv.at[q]
        )
    drain()

    def gather1(q):
        return (
            lambda yy, cc: slots_in.at[yy * 2 + cc, :, :, cols(q)], d_send.at[q], d_recv.at[q], e_send.at[q], e_recv.at[q]
        )

    for q in range(Q):
        wait_for(slots_in.at[n, :, :, cols(q)], c_recv.at[q])
        gather_start(*gather1(q))
    for q in range(Q):
        gather_forward(*gather1(q))

    for cp in loads[2:]:
        cp.wait()
    hid = None
    for q, (at, size) in enumerate(PARTS):
        gather_end(*gather1(q))
        rows_in = slots_in[:, :, :, cols(q)].reshape(256, size)
        term = jnp.dot(rows_in, win[cols(q), :], preferred_element_type=F32)
        hid = term if hid is None else hid + term
    first = lax.rem(lax.broadcasted_iota(jnp.int32, (256, 1), 0), OWN) < 4
    bias = b_in[...].astype(F32)
    hid = jnp.where(first, hid[:, :640] + bias[0:1], hid[:, 640:] + bias[1:2])
    hid = jax.nn.gelu(hid, approximate=True)
    hid = jnp.concatenate((jnp.where(first, hid, 0.0).astype(BF), jnp.where(first, 0.0, hid).astype(BF)), axis=1)
    for q, (at, size) in enumerate(PARTS):
        out = jnp.dot(hid, wout[:, cols(q)], preferred_element_type=F32)
        part[:, :, :, cols(q)] = out.astype(BF).reshape(NY, 2, 32, size)
        send(part.at[:, 1 - c, :, cols(q)], sib_part.at[:, :, cols(q)], f_send.at[q], f_recv.at[q], sib)
        own_part[:, :, :, cols(q)] = out.reshape(NY, 2, 32, size)

    for q, (at, size) in enumerate(PARTS):
        wait_for(sib_part.at[:, :, cols(q)], f_recv.at[q])
        for j in range(NY):
            chip = own_part[j, c, :, cols(q)] + sib_part[j, :, cols(q)].astype(F32)
            own2[j, :, cols(q)] = chip
            half2[j, :, cols(q)] = chip.astype(BF)
        for k in (2, 1, 3):
            send(
                half2.at[lax.rem(y + k, NY), :, cols(q)], far2.at[k - 1, :, cols(q)],
                g_send.at[q, k - 1], g_recv.at[q, k - 1], y_peer(k),
            )
    drain()
    bias = b_out[...].astype(F32)
    first = lax.rem(lax.broadcasted_iota(jnp.int32, (32, 1), 0), OWN) < 4
    bias = jnp.where(first, bias[0:1], bias[1:2])
    for q, (at, size) in enumerate(PARTS):
        for k in (1, 3, 2):
            wait_for(far2.at[k - 1, :, cols(q)], g_recv.at[q, k - 1])
        acc = own2[y, :, cols(q)] + bias[:, at:at + size]
        for k in range(3):
            acc = acc + far2[k, :, cols(q)].astype(F32)
        ready2[:, :, cols(q)] = acc.reshape(4, OWN, size).astype(BF)
        plane(
            lambda i: ready2.at[i, :, cols(q)], back.at[x, z // 4, lax.rem(z, 4), :, cols(q)], i_send.at[q], i_recv.at[q]
        )
    drain()

    def gather2(q):
        return (
            lambda yy, cc: back.at[lax.rem(yy + NX - x, NX), lax.rem(z // 4 + cc, 2), :, :, cols(q)],
            j_send.at[q], j_recv.at[q], k_send.at[q], k_recv.at[q],
        )

    for q in range(Q):
        wait_for(back.at[gx, h, :, :, cols(q)], i_recv.at[q])
        gather_start(*gather2(q))
    comb_out.wait()
    for q in range(Q):
        gather_forward(*gather2(q))
    for q in range(Q):
        gather_end(*gather2(q))
    drain()


def on_device(tokens, slot_keys, w_in, b_in, w_out, b_out):
    rows = tokens.shape[1]
    slots = NZ * NX * OWN
    hbm = pl.BlockSpec(memory_space=pltpu.HBM)
    anywhere = pl.BlockSpec(memory_space=pl.ANY)
    dma = pltpu.SemaphoreType.DMA
    block = (4, OWN, D)
    comb, back = pl.pallas_call(
        kernel,
        out_shape=(
            jax.ShapeDtypeStruct((rows, slots), BF),
            jax.ShapeDtypeStruct((NX, 2) + block, BF),
        ),
        in_specs=[hbm] * 6,
        out_specs=(anywhere, anywhere),
        scratch_shapes=[
            pltpu.VMEM((rows, D), BF),
            pltpu.VMEM((D, D), BF),
            pltpu.VMEM((D, D), BF),
            pltpu.VMEM((2, 640), BF),
            pltpu.VMEM((2, D), BF),
            pltpu.VMEM((OWN, D), BF),
            pltpu.VMEM((NX, 2) + block, BF),
            pltpu.VMEM((slots // 2, rows), F32),
            pltpu.VMEM((rows, slots), BF),
            pltpu.VMEM((NX, 32, D), BF),
            pltpu.VMEM((NX, 32, 128), F32),
            pltpu.VMEM((NX, 32, D), BF),
            pltpu.VMEM((NX, 32, 128), F32),
            pltpu.VMEM((NX, 32, D), F32),
            pltpu.VMEM((NX, 32, D), BF),
            pltpu.VMEM((NX, 32, 128), F32),
            pltpu.VMEM((3, 32, D), BF),
            pltpu.VMEM((3, 32, 128), F32),
            pltpu.VMEM(block, BF),
            pltpu.VMEM((8,) + block, BF),
            pltpu.VMEM((NY, 2, 32, D), BF),
            pltpu.VMEM((NY, 2, 32, D), F32),
            pltpu.VMEM((NY, 32, D), BF),
            pltpu.VMEM((NY, 32, D), BF),
            pltpu.VMEM((NY, 32, D), F32),
            pltpu.VMEM((3, 32, D), BF),
            pltpu.VMEM(block, BF),
            dma((8,)), dma((16,)), dma((4,)), dma((4,)), dma((4,)),
            dma, dma, dma((Q,)), dma((Q,)), dma((3,)), dma((3,)), dma((Q, 3)), dma((Q, 3)),
            dma((Q, 4)), dma((Q,)), dma((Q, 3)), dma((Q, 3)), dma((Q, 4)), dma((Q, 4)),
            dma((Q,)), dma((Q,)), dma((Q, 3)), dma((Q, 3)),
            dma((Q, 4)), dma((Q,)), dma((Q, 3)), dma((Q, 3)), dma((Q, 4)), dma((Q, 4)),
        ],
        compiler_params=pltpu.CompilerParams(
            collective_id=0, has_side_effects=True, vmem_limit_bytes=60 * 1024 * 1024
        ),
    )(tokens[0], slot_keys.T, w_in, b_in, w_out.reshape(-1, D), b_out)
    mixed = jnp.dot(comb, back.reshape(slots, D), preferred_element_type=F32)
    return mixed.astype(BF)[None]


def solution(mesh):
    in_specs = (
        P("wide", "narrow", None),
        P(None, "wide"),
        P("wide", None, "narrow"),
        P("wide", "narrow"),
        P("wide", "narrow", None),
        P("wide", None),
    )
    return jax.shard_map(
        on_device, mesh=mesh, in_specs=in_specs, out_specs=P("wide", "narrow", None), check_vma=False
    )
```

```python
import jax
import jax.numpy as jnp
from jax import lax
from jax.experimental import pallas as pl
from jax.experimental.pallas import tpu as pltpu
from jax.sharding import PartitionSpec as P

MESH = pl.DeviceIdType.MESH
BF = jnp.bfloat16
F32 = jnp.float32
NZ, NX, NY = 8, 4, 4
OWN = 8
D = 1280
PARTS = ((0, 640), (640, 640))
Q = len(PARTS)


def kernel(
    tok_hbm, key_hbm, win_hbm, bin_hbm, wout_hbm, bout_hbm,
    comb_ref, back,
    tok, tok_t, win, wout, b_in, b_out, own_key, keys, lt, comb,
    sums, stat, sib_sums, sib_stat, own_sums, half, half_stat, far, far_stat,
    ready, slots_in, part, own_part, sib_part, half2, far2, ready2,
    load_sem, key_send, key_recv, fwd_send, fwd_recv,
    as_send, as_recv, a_send, a_recv, bs_send, bs_recv, b_send, b_recv,
    c_send, c_recv, d_send, d_recv, e_send, e_recv,
    f_send, f_recv, g_send, g_recv, i_send, i_recv, j_send, j_recv, k_send, k_recv,
):
    w, n = lax.axis_index("wide"), lax.axis_index("narrow")
    z, x = w // NX, lax.rem(w, NX)
    y, c = n // 2, lax.rem(n, 2)
    sib = (w, y * 2 + 1 - c)
    h = lax.rem(z // 4 + c, 2)
    q_half = 1 - h
    gx = lax.rem(y + NX - x, NX)
    tokens = tok.shape[0]
    started = []

    def y_peer(k):
        return (w, lax.rem(y + k, NY) * 2 + c)

    def cols(q):
        return pl.ds(*PARTS[q])

    def remote(src, dst, s_sem, r_sem, dev):
        return pltpu.make_async_remote_copy(
            src_ref=src, dst_ref=dst, send_sem=s_sem, recv_sem=r_sem, device_id=dev, device_id_type=MESH
        )

    def send(src, dst, s_sem, r_sem, dev):
        cp = remote(src, dst, s_sem, r_sem, dev)
        cp.start()
        started.append((None, cp))

    def send_wide(src, dst, s_sem, r_sem, w_to):
        cp = remote(src, dst, s_sem, r_sem, (w_to, n))

        @pl.when(w_to != w)
        def _():
            cp.start()

        @pl.when(w_to == w)
        def _():
            pltpu.make_async_copy(src, dst, r_sem).start()

        started.append((w_to, cp))

    def drain():
        for w_to, cp in started:
            if w_to is None:
                cp.wait_send()
            else:
                @pl.when(w_to != w)
                def _():
                    cp.wait_send()
        started.clear()

    def wait_for(ref, sem):
        pltpu.make_async_copy(ref, ref, sem).wait()

    loads = [
        pltpu.make_async_copy(src, dst, load_sem.at[i])
        for i, (src, dst) in enumerate((
            (key_hbm, own_key), (tok_hbm, tok),
            (win_hbm.at[0], win.at[:, pl.ds(0, 640)]), (win_hbm.at[1], win.at[:, pl.ds(640, 640)]),
            (wout_hbm, wout), (bin_hbm, b_in), (bout_hbm, b_out),
        ))
    ]
    for cp in loads:
        cp.start()

    barrier = pltpu.get_barrier_semaphore()

    def greet(w_to, n_to):
        pl.semaphore_signal(barrier, inc=1, device_id=(w_to, n_to), device_id_type=MESH)

    key_peers = [(dx, (4 * q_half + i) * NX + lax.rem(x + dx, NX)) for dx in (2, 1, 3, 0) for i in range(4)]
    for dx, w_to in key_peers:
        if dx:
            greet(w_to, n)
        else:
            @pl.when(w_to != w)
            def _():
                greet(w_to, n)
    for k in (2, 1, 3):
        greet(*y_peer(k))
    greet(*sib)
    pl.semaphore_wait(barrier, 20 - c)
    loads[0].wait()

    for p, (dx, w_to) in enumerate(key_peers):
        dst = keys.at[x, z // 4, lax.rem(z, 4)]
        if dx:
            send(own_key, dst, key_send.at[p], key_recv.at[dx], (w_to, n))
        else:
            send_wide(own_key, dst, key_send.at[p], key_recv.at[dx], w_to)
    loads[1].wait()
    step = tokens // 9
    for i in range(9):
        tok_t[:, i * step:(i + 1) * step] = tok[i * step:(i + 1) * step, :].T
    for dx in (0, 1, 3, 2):
        got = keys.at[lax.rem(x + NX - dx, NX), q_half]
        wait_for(got, key_recv.at[dx])
        send(got, got, fwd_send.at[dx], fwd_recv.at[dx], sib)

    def column_softmax(half_index):
        key_rows = keys[:, half_index].reshape(128, D)
        for i in range(0, tokens, 256):
            to = min(tokens, i + 256)
            lt[:, i:to] = jnp.dot(key_rows, tok_t[:, i:to], preferred_element_type=F32)
        logits = lt[...]
        top = jnp.max(logits, axis=1, keepdims=True)
        spread = jnp.exp(logits - top)
        return top, jnp.sum(spread, axis=1, keepdims=True), spread.astype(BF)

    lane = lax.broadcasted_iota(jnp.int32, (128, 128), 1)
    top, totals, dispatch = column_softmax(q_half)
    stat[...] = jnp.where(lane < 64, top, totals).reshape(NX, 32, 128)
    send(stat, sib_stat, as_send, as_recv, sib)
    for q, (at, size) in enumerate(PARTS):
        sums[:, :, cols(q)] = (
            jnp.dot(dispatch, tok[:, cols(q)], preferred_element_type=F32).astype(BF).reshape(NX, 32, size)
        )
        send(sums.at[:, :, cols(q)], sib_sums.at[:, :, cols(q)], a_send.at[q], a_recv.at[q], sib)
    for dx in (0, 1, 3, 2):
        wait_for(keys.at[lax.rem(x + NX - dx, NX), h], fwd_recv.at[dx])
    top, totals, dispatch = column_softmax(h)
    wait_for(sib_stat, as_recv)
    other = sib_stat[...].reshape(128, 128)
    other_top, other_totals = other[:, 0:1], other[:, 64:65]
    chip_top = jnp.maximum(top, other_top)
    own_scale, other_scale = jnp.exp(top - chip_top), jnp.exp(other_top - chip_top)
    chip_totals = totals * own_scale + other_totals * other_scale
    half_stat[...] = jnp.where(lane < 64, chip_top, chip_totals).reshape(NX, 32, 128)
    for k in (2, 1, 3):
        to = lax.rem(y + k + NX - x, NX)
        send(half_stat.at[to], far_stat.at[k - 1], bs_send.at[k - 1], bs_recv.at[k - 1], y_peer(k))
    for q, (at, size) in enumerate(PARTS):
        mine = jnp.dot(dispatch, tok[:, cols(q)], preferred_element_type=F32) * own_scale
        wait_for(sib_sums.at[:, :, cols(q)], a_recv.at[q])
        chip = mine + sib_sums[:, :, cols(q)].astype(F32).reshape(128, size) * other_scale
        own_sums[:, :, cols(q)] = chip.reshape(NX, 32, size)
        half[:, :, cols(q)] = chip.astype(BF).reshape(NX, 32, size)
        for k in (2, 1, 3):
            to = lax.rem(y + k + NX - x, NX)
            send(half.at[to, :, cols(q)], far.at[k - 1, :, cols(q)], b_send.at[q, k - 1], b_recv.at[q, k - 1], y_peer(k))

    key_rows = keys[...].reshape(256, D)
    for i in range(4):
        rows = slice(i * (tokens // 4), (i + 1) * (tokens // 4))
        logits = lax.dot_general(
            tok[rows, :], key_rows, (((1,), (1,)), ((), ())), preferred_element_type=F32
        )
        row_spread = jnp.exp(logits - jnp.max(logits, axis=1, keepdims=True))
        comb[rows, :] = (row_spread / jnp.sum(row_spread, axis=1, keepdims=True)).astype(BF)
    comb_out = pltpu.make_async_copy(comb, comb_ref, load_sem.at[7])
    comb_out.start()

    for k in (1, 3, 2):
        wait_for(far_stat.at[k - 1], bs_recv.at[k - 1])
    st = [half_stat[gx]] + [far_stat[k] for k in range(3)]
    ms = [s[:, 0:1] for s in st]
    ts = [s[:, 64:65] for s in st]
    m = jnp.maximum(jnp.maximum(ms[0], ms[1]), jnp.maximum(ms[2], ms[3]))
    fs = [jnp.exp(mi - m) for mi in ms]
    inv = 1.0 / (ts[0] * fs[0] + ts[1] * fs[1] + ts[2] * fs[2] + ts[3] * fs[3])
    fs = [f * inv for f in fs]

    def plane(src, there, s_sem, r_sem):
        for i in range(4):
            send_wide(src(i), there, s_sem.at[i], r_sem, (4 * h + i) * NX + gx)

    def gather_start(place, y_send, y_recv, s_send, s_recv):
        own = place(y, c)
        for k in (2, 1, 3):
            send(own, own, y_send.at[k - 1], y_recv.at[k - 1], y_peer(k))
        send(own, own, s_send.at[0], s_recv.at[0], sib)

    def gather_forward(place, y_send, y_recv, s_send, s_recv):
        for k in (1, 3, 2):
            got = place(lax.rem(y + NY - k, NY), c)
            wait_for(got, y_recv.at[k - 1])
            send(got, got, s_send.at[k], s_recv.at[k], sib)

    def gather_end(place, y_send, y_recv, s_send, s_recv):
        for k in range(NY):
            wait_for(place(lax.rem(y + NY - k, NY), 1 - c), s_recv.at[k])

    for q, (at, size) in enumerate(PARTS):
        for k in (1, 3, 2):
            wait_for(far.at[k - 1, :, cols(q)], b_recv.at[q, k - 1])
        acc = own_sums[gx, :, cols(q)] * fs[0]
        for k in range(3):
            acc = acc + far[k, :, cols(q)].astype(F32) * fs[k + 1]
        ready[:, :, cols(q)] = acc.reshape(4, OWN, size).astype(BF)
        plane(
            lambda i: ready.at[i, :, cols(q)], slots_in.at[y, c, lax.rem(z, 4), :, cols(q)], c_send.at[q], c_recv.at[q]
        )
    drain()

    def gather1(q):
        return (
            lambda yy, cc: slots_in.at[yy, cc, :, :, cols(q)], d_send.at[q], d_recv.at[q], e_send.at[q], e_recv.at[q]
        )

    for q in range(Q):
        wait_for(slots_in.at[y, c, :, :, cols(q)], c_recv.at[q])
        gather_start(*gather1(q))
    for q in range(Q):
        gather_forward(*gather1(q))

    for cp in loads[2:]:
        cp.wait()
    first = lax.rem(lax.broadcasted_iota(jnp.int32, (128, 1), 0), OWN) < 4
    bias = b_in[...].astype(F32)

    def hidden(core):
        hid = None
        for q, (at, size) in enumerate(PARTS):
            rows_in = slots_in[:, core, :, :, cols(q)].reshape(128, size)
            term = jnp.dot(rows_in, win[cols(q), :], preferred_element_type=F32)
            hid = term if hid is None else hid + term
        hid = jnp.where(first, hid[:, :640] + bias[0:1], hid[:, 640:] + bias[1:2])
        hid = jax.nn.gelu(hid, approximate=True)
        return jnp.concatenate((jnp.where(first, hid, 0.0).astype(BF), jnp.where(first, 0.0, hid).astype(BF)), axis=1)

    hid_c = hidden(c)
    for q in range(Q):
        gather_end(*gather1(q))
    hid_sib = hidden(1 - c)
    for q, (at, size) in enumerate(PARTS):
        out = jnp.dot(hid_sib, wout[:, cols(q)], preferred_element_type=F32)
        part[:, :, cols(q)] = out.astype(BF).reshape(NY, 32, size)
        send(part.at[:, :, cols(q)], sib_part.at[:, :, cols(q)], f_send.at[q], f_recv.at[q], sib)
    for q, (at, size) in enumerate(PARTS):
        out = jnp.dot(hid_c, wout[:, cols(q)], preferred_element_type=F32)
        own_part[:, :, cols(q)] = out.reshape(NY, 32, size)

    for q, (at, size) in enumerate(PARTS):
        wait_for(sib_part.at[:, :, cols(q)], f_recv.at[q])
        chip = own_part[:, :, cols(q)] + sib_part[:, :, cols(q)].astype(F32)
        own_part[:, :, cols(q)] = chip
        half2[:, :, cols(q)] = chip.astype(BF)
        for k in (2, 1, 3):
            send(
                half2.at[lax.rem(y + k, NY), :, cols(q)], far2.at[k - 1, :, cols(q)],
                g_send.at[q, k - 1], g_recv.at[q, k - 1], y_peer(k),
            )
    drain()
    bias = b_out[...].astype(F32)
    first = lax.rem(lax.broadcasted_iota(jnp.int32, (32, 1), 0), OWN) < 4
    bias = jnp.where(first, bias[0:1], bias[1:2])
    for q, (at, size) in enumerate(PARTS):
        for k in (1, 3, 2):
            wait_for(far2.at[k - 1, :, cols(q)], g_recv.at[q, k - 1])
        acc = own_part[y, :, cols(q)] + bias[:, at:at + size]
        for k in range(3):
            acc = acc + far2[k, :, cols(q)].astype(F32)
        ready2[:, :, cols(q)] = acc.reshape(4, OWN, size).astype(BF)
        plane(
            lambda i: ready2.at[i, :, cols(q)], back.at[x, z // 4, lax.rem(z, 4), :, cols(q)], i_send.at[q], i_recv.at[q]
        )
    drain()

    def gather2(q):
        return (
            lambda yy, cc: back.at[lax.rem(yy + NX - x, NX), lax.rem(z // 4 + cc, 2), :, :, cols(q)],
            j_send.at[q], j_recv.at[q], k_send.at[q], k_recv.at[q],
        )

    for q in range(Q):
        wait_for(back.at[gx, h, :, :, cols(q)], i_recv.at[q])
        gather_start(*gather2(q))
    comb_out.wait()
    for q in range(Q):
        gather_forward(*gather2(q))
    for q in range(Q):
        gather_end(*gather2(q))
    drain()


def on_device(tokens, slot_keys, w_in, b_in, w_out, b_out):
    rows = tokens.shape[1]
    slots = NZ * NX * OWN
    hbm = pl.BlockSpec(memory_space=pltpu.HBM)
    anywhere = pl.BlockSpec(memory_space=pl.ANY)
    dma = pltpu.SemaphoreType.DMA
    block = (4, OWN, D)
    comb, back = pl.pallas_call(
        kernel,
        out_shape=(
            pltpu.VMEM((rows, slots), BF),
            pltpu.VMEM((NX, 2) + block, BF),
        ),
        in_specs=[hbm] * 6,
        out_specs=(anywhere, anywhere),
        scratch_shapes=[
            pltpu.VMEM((rows, D), BF),
            pltpu.VMEM((D, rows), BF),
            pltpu.VMEM((D, D), BF),
            pltpu.VMEM((D, D), BF),
            pltpu.VMEM((2, 640), BF),
            pltpu.VMEM((2, D), BF),
            pltpu.VMEM((OWN, D), BF),
            pltpu.VMEM((NX, 2) + block, BF),
            pltpu.VMEM((slots // 2, rows), F32),
            pltpu.VMEM((rows, slots), BF),
            pltpu.VMEM((NX, 32, D), BF),
            pltpu.VMEM((NX, 32, 128), F32),
            pltpu.VMEM((NX, 32, D), BF),
            pltpu.VMEM((NX, 32, 128), F32),
            pltpu.VMEM((NX, 32, D), F32),
            pltpu.VMEM((NX, 32, D), BF),
            pltpu.VMEM((NX, 32, 128), F32),
            pltpu.VMEM((3, 32, D), BF),
            pltpu.VMEM((3, 32, 128), F32),
            pltpu.VMEM(block, BF),
            pltpu.VMEM((NY, 2) + block, BF),
            pltpu.VMEM((NY, 32, D), BF),
            pltpu.VMEM((NY, 32, D), F32),
            pltpu.VMEM((NY, 32, D), BF),
            pltpu.VMEM((NY, 32, D), BF),
            pltpu.VMEM((3, 32, D), BF),
            pltpu.VMEM(block, BF),
            dma((8,)), dma((16,)), dma((4,)), dma((4,)), dma((4,)),
            dma, dma, dma((Q,)), dma((Q,)), dma((3,)), dma((3,)), dma((Q, 3)), dma((Q, 3)),
            dma((Q, 4)), dma((Q,)), dma((Q, 3)), dma((Q, 3)), dma((Q, 4)), dma((Q, 4)),
            dma((Q,)), dma((Q,)), dma((Q, 3)), dma((Q, 3)),
            dma((Q, 4)), dma((Q,)), dma((Q, 3)), dma((Q, 3)), dma((Q, 4)), dma((Q, 4)),
        ],
        compiler_params=pltpu.CompilerParams(
            collective_id=0, has_side_effects=True, vmem_limit_bytes=48 * 1024 * 1024
        ),
    )(*(
        pltpu.with_memory_space_constraint(a, pltpu.HBM)
        for a in (tokens[0], slot_keys.T, w_in, b_in, w_out.reshape(-1, D), b_out)
    ))
    mixed = jnp.dot(comb, back.reshape(slots, D), preferred_element_type=F32)
    return mixed.astype(BF)[None]


def solution(mesh):
    in_specs = (
        P("wide", "narrow", None),
        P(None, "wide"),
        P("wide", None, "narrow"),
        P("wide", "narrow"),
        P("wide", "narrow", None),
        P("wide", None),
    )
    return jax.shard_map(
        on_device, mesh=mesh, in_specs=in_specs, out_specs=P("wide", "narrow", None), check_vma=False
    )
```

```python
import jax
import jax.numpy as jnp
from jax import lax
from jax.experimental import pallas as pl
from jax.experimental.pallas import tpu as pltpu
from jax.sharding import PartitionSpec as P

MESH = pl.DeviceIdType.MESH
BF = jnp.bfloat16
F32 = jnp.float32
NZ, NX, NY = 8, 4, 4
OWN = 8
D = 1280
PARTS = ((0, 640), (640, 640))
Q = len(PARTS)
MIX_STEPS = 6


def kernel(
    tok_hbm, key_hbm, win_hbm, bin_hbm, wout_hbm, bout_hbm,
    comb_ref, back,
    tok, tok_t, win, wout, b_in, b_out, own_key, keys, lt, comb,
    sums, stat, sib_sums, sib_stat, own_sums, half, half_stat, far, far_stat,
    ready, slots_in, part, own_part, sib_part, half2, far2, ready2,
    load_sem, key_send, key_recv, fwd_send, fwd_recv,
    as_send, as_recv, a_send, a_recv, bs_send, bs_recv, b_send, b_recv,
    c_send, c_recv, d_send, d_recv, e_send, e_recv,
    f_send, f_recv, g_send, g_recv, i_send, i_recv, j_send, j_recv, k_send, k_recv,
):
    w, n = lax.axis_index("wide"), lax.axis_index("narrow")
    z, x = w // NX, lax.rem(w, NX)
    y, c = n // 2, lax.rem(n, 2)
    sib = (w, y * 2 + 1 - c)
    h = lax.rem(z // 4 + c, 2)
    q_half = 1 - h
    gx = lax.rem(y + NX - x, NX)
    tokens = tok.shape[0]
    started = []

    def y_peer(k):
        return (w, lax.rem(y + k, NY) * 2 + c)

    def cols(q):
        return pl.ds(*PARTS[q])

    def remote(src, dst, s_sem, r_sem, dev):
        return pltpu.make_async_remote_copy(
            src_ref=src, dst_ref=dst, send_sem=s_sem, recv_sem=r_sem, device_id=dev, device_id_type=MESH
        )

    def send(src, dst, s_sem, r_sem, dev):
        cp = remote(src, dst, s_sem, r_sem, dev)
        cp.start()
        started.append((None, cp))

    def send_wide(src, dst, s_sem, r_sem, w_to):
        cp = remote(src, dst, s_sem, r_sem, (w_to, n))

        @pl.when(w_to != w)
        def _():
            cp.start()

        @pl.when(w_to == w)
        def _():
            pltpu.make_async_copy(src, dst, r_sem).start()

        started.append((w_to, cp))

    def drain(count):
        for w_to, cp in started[:count]:
            if w_to is None:
                cp.wait_send()
            else:
                @pl.when(w_to != w)
                def _():
                    cp.wait_send()
        del started[:count]

    def wait_for(ref, sem):
        pltpu.make_async_copy(ref, ref, sem).wait()

    loads = [
        pltpu.make_async_copy(src, dst, load_sem.at[i])
        for i, (src, dst) in enumerate((
            (key_hbm, own_key), (tok_hbm, tok),
            (win_hbm.at[0], win.at[:, pl.ds(0, 640)]), (win_hbm.at[1], win.at[:, pl.ds(640, 640)]),
            (wout_hbm, wout), (bin_hbm, b_in), (bout_hbm, b_out),
        ))
    ]
    barrier = pltpu.get_barrier_semaphore()

    def greet(w_to, n_to):
        pl.semaphore_signal(barrier, inc=1, device_id=(w_to, n_to), device_id_type=MESH)

    key_peers = [(dx, (4 * q_half + i) * NX + lax.rem(x + dx, NX)) for dx in (2, 1, 3, 0) for i in range(4)]
    for dx, w_to in key_peers:
        if dx:
            greet(w_to, n)
        else:
            @pl.when(w_to != w)
            def _():
                greet(w_to, n)
    for k in (2, 1, 3):
        greet(*y_peer(k))
    greet(*sib)
    for cp in loads:
        cp.start()
    pl.semaphore_wait(barrier, 20 - c)
    loads[0].wait()

    for p, (dx, w_to) in enumerate(key_peers):
        dst = keys.at[x, z // 4, lax.rem(z, 4)]
        if dx:
            send(own_key, dst, key_send.at[p], key_recv.at[dx], (w_to, n))
        else:
            send_wide(own_key, dst, key_send.at[p], key_recv.at[dx], w_to)
    loads[1].wait()
    step = tokens // 9
    for i in range(9):
        tok_t[:, i * step:(i + 1) * step] = tok[i * step:(i + 1) * step, :].T
    for dx in (0, 1, 3, 2):
        got = keys.at[lax.rem(x + NX - dx, NX), q_half]
        wait_for(got, key_recv.at[dx])
        send(got, got, fwd_send.at[dx], fwd_recv.at[dx], sib)

    def column_softmax(half_index):
        key_rows = keys[:, half_index].reshape(128, D)
        for i in range(0, tokens, 256):
            to = min(tokens, i + 256)
            lt[:, i:to] = jnp.dot(key_rows, tok_t[:, i:to], preferred_element_type=F32)
        logits = lt[...]
        top = jnp.max(logits, axis=1, keepdims=True)
        spread = jnp.exp(logits - top)
        return top, jnp.sum(spread, axis=1, keepdims=True), spread.astype(BF)

    lane = lax.broadcasted_iota(jnp.int32, (128, 128), 1)
    top, totals, dispatch = column_softmax(q_half)
    stat[...] = jnp.where(lane < 64, top, totals).reshape(NX, 32, 128)
    send(stat, sib_stat, as_send, as_recv, sib)
    for q, (at, size) in enumerate(PARTS):
        sums[:, :, cols(q)] = (
            jnp.dot(dispatch, tok[:, cols(q)], preferred_element_type=F32).astype(BF).reshape(NX, 32, size)
        )
        send(sums.at[:, :, cols(q)], sib_sums.at[:, :, cols(q)], a_send.at[q], a_recv.at[q], sib)
    for dx in (0, 1, 3, 2):
        wait_for(keys.at[lax.rem(x + NX - dx, NX), h], fwd_recv.at[dx])
    top, totals, dispatch = column_softmax(h)
    wait_for(sib_stat, as_recv)
    other = sib_stat[...].reshape(128, 128)
    other_top, other_totals = other[:, 0:1], other[:, 64:65]
    chip_top = jnp.maximum(top, other_top)
    own_scale, other_scale = jnp.exp(top - chip_top), jnp.exp(other_top - chip_top)
    chip_totals = totals * own_scale + other_totals * other_scale
    half_stat[...] = jnp.where(lane < 64, chip_top, chip_totals).reshape(NX, 32, 128)
    for k in (2, 1, 3):
        to = lax.rem(y + k + NX - x, NX)
        send(half_stat.at[to], far_stat.at[k - 1], bs_send.at[k - 1], bs_recv.at[k - 1], y_peer(k))
    for q, (at, size) in enumerate(PARTS):
        mine = jnp.dot(dispatch, tok[:, cols(q)], preferred_element_type=F32) * own_scale
        wait_for(sib_sums.at[:, :, cols(q)], a_recv.at[q])
        chip = mine + sib_sums[:, :, cols(q)].astype(F32).reshape(128, size) * other_scale
        own_sums[:, :, cols(q)] = chip.reshape(NX, 32, size)
        half[:, :, cols(q)] = chip.astype(BF).reshape(NX, 32, size)
        for k in (2, 1, 3):
            to = lax.rem(y + k + NX - x, NX)
            send(half.at[to, :, cols(q)], far.at[k - 1, :, cols(q)], b_send.at[q, k - 1], b_recv.at[q, k - 1], y_peer(k))

    key_rows = keys[...].reshape(256, D)
    for i in range(4):
        rows = slice(i * (tokens // 4), (i + 1) * (tokens // 4))
        logits = lax.dot_general(
            tok[rows, :], key_rows, (((1,), (1,)), ((), ())), preferred_element_type=F32
        )
        row_spread = jnp.exp(logits - jnp.max(logits, axis=1, keepdims=True))
        comb[rows, :] = (row_spread / jnp.sum(row_spread, axis=1, keepdims=True)).astype(BF)
    comb_out = pltpu.make_async_copy(comb, comb_ref, load_sem.at[7])
    comb_out.start()

    for k in (1, 3, 2):
        wait_for(far_stat.at[k - 1], bs_recv.at[k - 1])
    st = [half_stat[gx]] + [far_stat[k] for k in range(3)]
    ms = [s[:, 0:1] for s in st]
    ts = [s[:, 64:65] for s in st]
    m = jnp.maximum(jnp.maximum(ms[0], ms[1]), jnp.maximum(ms[2], ms[3]))
    fs = [jnp.exp(mi - m) for mi in ms]
    inv = 1.0 / (ts[0] * fs[0] + ts[1] * fs[1] + ts[2] * fs[2] + ts[3] * fs[3])
    fs = [f * inv for f in fs]

    def plane(src, there, s_sem, r_sem):
        for i in range(4):
            send_wide(src(i), there, s_sem.at[i], r_sem, (4 * h + i) * NX + gx)

    def gather_start(place, y_send, y_recv, s_send, s_recv):
        own = place(y, c)
        for k in (2, 1, 3):
            send(own, own, y_send.at[k - 1], y_recv.at[k - 1], y_peer(k))
        send(own, own, s_send.at[0], s_recv.at[0], sib)

    def gather_forward(place, y_send, y_recv, s_send, s_recv):
        for k in (1, 3, 2):
            got = place(lax.rem(y + NY - k, NY), c)
            wait_for(got, y_recv.at[k - 1])
            send(got, got, s_send.at[k], s_recv.at[k], sib)

    def gather_end(place, y_send, y_recv, s_send, s_recv):
        for k in range(NY):
            wait_for(place(lax.rem(y + NY - k, NY), 1 - c), s_recv.at[k])

    before = len(started)
    for q, (at, size) in enumerate(PARTS):
        for k in (1, 3, 2):
            wait_for(far.at[k - 1, :, cols(q)], b_recv.at[q, k - 1])
        acc = own_sums[gx, :, cols(q)] * fs[0]
        for k in range(3):
            acc = acc + far[k, :, cols(q)].astype(F32) * fs[k + 1]
        ready[:, :, cols(q)] = acc.reshape(4, OWN, size).astype(BF)
        plane(
            lambda i: ready.at[i, :, cols(q)], slots_in.at[y, c, lax.rem(z, 4), :, cols(q)], c_send.at[q], c_recv.at[q]
        )
    drain(before)

    def gather1(q):
        return (
            lambda yy, cc: slots_in.at[yy, cc, :, :, cols(q)], d_send.at[q], d_recv.at[q], e_send.at[q], e_recv.at[q]
        )

    for q in range(Q):
        wait_for(slots_in.at[y, c, :, :, cols(q)], c_recv.at[q])
        gather_start(*gather1(q))
    for q in range(Q):
        gather_forward(*gather1(q))

    for cp in loads[2:]:
        cp.wait()
    first = lax.rem(lax.broadcasted_iota(jnp.int32, (128, 1), 0), OWN) < 4
    bias = b_in[...].astype(F32)

    def hidden(core):
        hid = None
        for q, (at, size) in enumerate(PARTS):
            rows_in = slots_in[:, core, :, :, cols(q)].reshape(128, size)
            term = jnp.dot(rows_in, win[cols(q), :], preferred_element_type=F32)
            hid = term if hid is None else hid + term
        hid = jnp.where(first, hid[:, :640] + bias[0:1], hid[:, 640:] + bias[1:2])
        hid = jax.nn.gelu(hid, approximate=True)
        return jnp.concatenate((jnp.where(first, hid, 0.0).astype(BF), jnp.where(first, 0.0, hid).astype(BF)), axis=1)

    hid_c = hidden(c)
    for q in range(Q):
        gather_end(*gather1(q))
    hid_sib = hidden(1 - c)
    for q, (at, size) in enumerate(PARTS):
        out = jnp.dot(hid_sib, wout[:, cols(q)], preferred_element_type=F32)
        part[:, :, cols(q)] = out.astype(BF).reshape(NY, 32, size)
        send(part.at[:, :, cols(q)], sib_part.at[:, :, cols(q)], f_send.at[q], f_recv.at[q], sib)
    for q, (at, size) in enumerate(PARTS):
        out = jnp.dot(hid_c, wout[:, cols(q)], preferred_element_type=F32)
        own_part[:, :, cols(q)] = out.reshape(NY, 32, size)

    before = len(started)
    for q, (at, size) in enumerate(PARTS):
        wait_for(sib_part.at[:, :, cols(q)], f_recv.at[q])
        chip = own_part[:, :, cols(q)] + sib_part[:, :, cols(q)].astype(F32)
        own_part[:, :, cols(q)] = chip
        half2[:, :, cols(q)] = chip.astype(BF)
        for k in (2, 1, 3):
            send(
                half2.at[lax.rem(y + k, NY), :, cols(q)], far2.at[k - 1, :, cols(q)],
                g_send.at[q, k - 1], g_recv.at[q, k - 1], y_peer(k),
            )
    drain(before)
    bias = b_out[...].astype(F32)
    first = lax.rem(lax.broadcasted_iota(jnp.int32, (32, 1), 0), OWN) < 4
    bias = jnp.where(first, bias[0:1], bias[1:2])
    before = len(started)
    for q, (at, size) in enumerate(PARTS):
        for k in (1, 3, 2):
            wait_for(far2.at[k - 1, :, cols(q)], g_recv.at[q, k - 1])
        acc = own_part[y, :, cols(q)] + bias[:, at:at + size]
        for k in range(3):
            acc = acc + far2[k, :, cols(q)].astype(F32)
        ready2[:, :, cols(q)] = acc.reshape(4, OWN, size).astype(BF)
        plane(
            lambda i: ready2.at[i, :, cols(q)], back.at[x, z // 4, lax.rem(z, 4), :, cols(q)], i_send.at[q], i_recv.at[q]
        )
    drain(before)

    def gather2(q):
        return (
            lambda yy, cc: back.at[lax.rem(yy + NX - x, NX), lax.rem(z // 4 + cc, 2), :, :, cols(q)],
            j_send.at[q], j_recv.at[q], k_send.at[q], k_recv.at[q],
        )

    for q in range(Q):
        wait_for(back.at[gx, h, :, :, cols(q)], i_recv.at[q])
        gather_start(*gather2(q))
    comb_out.wait()
    before = len(started)
    for q in range(Q):
        gather_forward(*gather2(q))
    drain(before)
    for q in range(Q):
        gather_end(*gather2(q))
    drain(len(started))


def mix(comb, slot_out, out_ref, out, sem):
    step = out.shape[0] // MIX_STEPS
    copies = []
    for i in range(MIX_STEPS):
        rows = pl.ds(i * step, step)
        out[rows, :] = jnp.dot(comb[rows, :], slot_out[...], preferred_element_type=F32).astype(BF)
        cp = pltpu.make_async_copy(out.at[rows], out_ref.at[rows], sem.at[i])
        cp.start()
        copies.append(cp)
    for cp in copies:
        cp.wait()


def on_device(tokens, slot_keys, w_in, b_in, w_out, b_out):
    rows = tokens.shape[1]
    slots = NZ * NX * OWN
    hbm = pl.BlockSpec(memory_space=pltpu.HBM)
    anywhere = pl.BlockSpec(memory_space=pl.ANY)
    dma = pltpu.SemaphoreType.DMA
    block = (4, OWN, D)
    comb, back = pl.pallas_call(
        kernel,
        out_shape=(
            pltpu.VMEM((rows, slots), BF),
            pltpu.VMEM((NX, 2) + block, BF),
        ),
        in_specs=[hbm] * 6,
        out_specs=(anywhere, anywhere),
        scratch_shapes=[
            pltpu.VMEM((rows, D), BF),
            pltpu.VMEM((D, rows), BF),
            pltpu.VMEM((D, D), BF),
            pltpu.VMEM((D, D), BF),
            pltpu.VMEM((2, 640), BF),
            pltpu.VMEM((2, D), BF),
            pltpu.VMEM((OWN, D), BF),
            pltpu.VMEM((NX, 2) + block, BF),
            pltpu.VMEM((slots // 2, rows), F32),
            pltpu.VMEM((rows, slots), BF),
            pltpu.VMEM((NX, 32, D), BF),
            pltpu.VMEM((NX, 32, 128), F32),
            pltpu.VMEM((NX, 32, D), BF),
            pltpu.VMEM((NX, 32, 128), F32),
            pltpu.VMEM((NX, 32, D), F32),
            pltpu.VMEM((NX, 32, D), BF),
            pltpu.VMEM((NX, 32, 128), F32),
            pltpu.VMEM((3, 32, D), BF),
            pltpu.VMEM((3, 32, 128), F32),
            pltpu.VMEM(block, BF),
            pltpu.VMEM((NY, 2) + block, BF),
            pltpu.VMEM((NY, 32, D), BF),
            pltpu.VMEM((NY, 32, D), F32),
            pltpu.VMEM((NY, 32, D), BF),
            pltpu.VMEM((NY, 32, D), BF),
            pltpu.VMEM((3, 32, D), BF),
            pltpu.VMEM(block, BF),
            dma((8,)), dma((16,)), dma((4,)), dma((4,)), dma((4,)),
            dma, dma, dma((Q,)), dma((Q,)), dma((3,)), dma((3,)), dma((Q, 3)), dma((Q, 3)),
            dma((Q, 4)), dma((Q,)), dma((Q, 3)), dma((Q, 3)), dma((Q, 4)), dma((Q, 4)),
            dma((Q,)), dma((Q,)), dma((Q, 3)), dma((Q, 3)),
            dma((Q, 4)), dma((Q,)), dma((Q, 3)), dma((Q, 3)), dma((Q, 4)), dma((Q, 4)),
        ],
        compiler_params=pltpu.CompilerParams(
            collective_id=0, has_side_effects=True, vmem_limit_bytes=48 * 1024 * 1024
        ),
    )(*(
        pltpu.with_memory_space_constraint(a, pltpu.HBM)
        for a in (tokens[0], slot_keys.T, w_in, b_in, w_out.reshape(-1, D), b_out)
    ))
    vmem = pl.BlockSpec(memory_space=pltpu.VMEM)
    return pl.pallas_call(
        mix,
        out_shape=jax.ShapeDtypeStruct((rows, D), BF),
        in_specs=[vmem, vmem],
        out_specs=anywhere,
        scratch_shapes=[pltpu.VMEM((rows, D), BF), dma((MIX_STEPS,))],
        compiler_params=pltpu.CompilerParams(vmem_limit_bytes=32 * 1024 * 1024),
    )(
        pltpu.with_memory_space_constraint(comb, pltpu.VMEM),
        pltpu.with_memory_space_constraint(back.reshape(slots, D), pltpu.VMEM),
    )[None]


def solution(mesh):
    in_specs = (
        P("wide", "narrow", None),
        P(None, "wide"),
        P("wide", None, "narrow"),
        P("wide", "narrow"),
        P("wide", "narrow", None),
        P("wide", None),
    )
    return jax.shard_map(
        on_device, mesh=mesh, in_specs=in_specs, out_specs=P("wide", "narrow", None), check_vma=False
    )
```

```python
import jax
import jax.numpy as jnp
from jax import lax
from jax.experimental import pallas as pl
from jax.experimental.pallas import tpu as pltpu
from jax.sharding import PartitionSpec as P

MESH = pl.DeviceIdType.MESH
BF = jnp.bfloat16
F32 = jnp.float32
NZ, NX, NY = 8, 4, 4
OWN = 8
D = 1280
PARTS = ((0, 640), (640, 640))
Q = len(PARTS)
MIX_STEPS = 6


def kernel(
    tok_hbm, key_hbm, win_hbm, bin_hbm, wout_hbm, bout_hbm,
    comb_ref, back,
    tok, tok_t, win, wout, b_in, b_out, own_key, keys, lt, comb,
    sums, stat, sib_sums, sib_stat, own_sums, half, half_stat, far, far_stat,
    ready, slots_in, part, own_part, sib_part, half2, far2, ready2,
    load_sem, key_send, key_recv, fwd_send, fwd_recv,
    as_send, as_recv, a_send, a_recv, bs_send, bs_recv, b_send, b_recv,
    c_send, c_recv, d_send, d_recv, e_send, e_recv,
    f_send, f_recv, g_send, g_recv, i_send, i_recv, j_send, j_recv, k_send, k_recv,
):
    w, n = lax.axis_index("wide"), lax.axis_index("narrow")
    z, x = w // NX, lax.rem(w, NX)
    y, c = n // 2, lax.rem(n, 2)
    sib = (w, y * 2 + 1 - c)
    h = lax.rem(z // 4 + c, 2)
    q_half = 1 - h
    gx = lax.rem(y + NX - x, NX)
    tokens = tok.shape[0]
    started = []

    def y_peer(k):
        return (w, lax.rem(y + k, NY) * 2 + c)

    def cols(q):
        return pl.ds(*PARTS[q])

    def remote(src, dst, s_sem, r_sem, dev):
        return pltpu.make_async_remote_copy(
            src_ref=src, dst_ref=dst, send_sem=s_sem, recv_sem=r_sem, device_id=dev, device_id_type=MESH
        )

    def send(src, dst, s_sem, r_sem, dev):
        cp = remote(src, dst, s_sem, r_sem, dev)
        cp.start()
        started.append((None, cp))

    def send_wide(src, dst, s_sem, r_sem, w_to):
        cp = remote(src, dst, s_sem, r_sem, (w_to, n))

        @pl.when(w_to != w)
        def _():
            cp.start()

        @pl.when(w_to == w)
        def _():
            pltpu.make_async_copy(src, dst, r_sem).start()

        started.append((w_to, cp))

    def drain(count):
        for w_to, cp in started[:count]:
            if w_to is None:
                cp.wait_send()
            else:
                @pl.when(w_to != w)
                def _():
                    cp.wait_send()
        del started[:count]

    def wait_for(ref, sem):
        pltpu.make_async_copy(ref, ref, sem).wait()

    loads = [
        pltpu.make_async_copy(src, dst, load_sem.at[i])
        for i, (src, dst) in enumerate((
            (key_hbm, own_key), (tok_hbm, tok),
            (win_hbm.at[0], win.at[:, pl.ds(0, 640)]), (win_hbm.at[1], win.at[:, pl.ds(640, 640)]),
            (wout_hbm, wout), (bin_hbm, b_in), (bout_hbm, b_out),
        ))
    ]
    barrier = pltpu.get_barrier_semaphore()

    def greet(w_to, n_to):
        pl.semaphore_signal(barrier, inc=1, device_id=(w_to, n_to), device_id_type=MESH)

    key_peers = [(dx, (4 * q_half + i) * NX + lax.rem(x + dx, NX)) for dx in (2, 1, 3, 0) for i in range(4)]
    for dx, w_to in key_peers:
        if dx:
            greet(w_to, n)
        else:
            @pl.when(w_to != w)
            def _():
                greet(w_to, n)
    for k in (2, 1, 3):
        greet(*y_peer(k))
    greet(*sib)
    for cp in loads:
        cp.start()
    pl.semaphore_wait(barrier, 20 - c)
    loads[0].wait()

    for p, (dx, w_to) in enumerate(key_peers):
        dst = keys.at[x, z // 4, lax.rem(z, 4)]
        if dx:
            send(own_key, dst, key_send.at[p], key_recv.at[dx], (w_to, n))
        else:
            send_wide(own_key, dst, key_send.at[p], key_recv.at[dx], w_to)
    loads[1].wait()
    step = tokens // 9
    for i in range(9):
        tok_t[:, i * step:(i + 1) * step] = tok[i * step:(i + 1) * step, :].T
    for dx in (0, 1, 3, 2):
        got = keys.at[lax.rem(x + NX - dx, NX), q_half]
        wait_for(got, key_recv.at[dx])
        send(got, got, fwd_send.at[dx], fwd_recv.at[dx], sib)

    def column_softmax(half_index):
        key_rows = keys[:, half_index].reshape(128, D)
        for i in range(0, tokens, 256):
            to = min(tokens, i + 256)
            lt[:, i:to] = jnp.dot(key_rows, tok_t[:, i:to], preferred_element_type=F32)
        logits = lt[...]
        top = jnp.max(logits, axis=1, keepdims=True)
        spread = jnp.exp(logits - top)
        return top, jnp.sum(spread, axis=1, keepdims=True), spread.astype(BF)

    lane = lax.broadcasted_iota(jnp.int32, (128, 128), 1)
    top, totals, dispatch = column_softmax(q_half)
    stat[...] = jnp.where(lane < 64, top, totals).reshape(NX, 32, 128)
    send(stat, sib_stat, as_send, as_recv, sib)
    for q, (at, size) in enumerate(PARTS):
        sums[:, :, cols(q)] = (
            jnp.dot(dispatch, tok[:, cols(q)], preferred_element_type=F32).astype(BF).reshape(NX, 32, size)
        )
        send(sums.at[:, :, cols(q)], sib_sums.at[:, :, cols(q)], a_send.at[q], a_recv.at[q], sib)
    for dx in (0, 1, 3, 2):
        wait_for(keys.at[lax.rem(x + NX - dx, NX), h], fwd_recv.at[dx])
    top, totals, dispatch = column_softmax(h)
    wait_for(sib_stat, as_recv)
    other = sib_stat[...].reshape(128, 128)
    other_top, other_totals = other[:, 0:1], other[:, 64:65]
    chip_top = jnp.maximum(top, other_top)
    own_scale, other_scale = jnp.exp(top - chip_top), jnp.exp(other_top - chip_top)
    chip_totals = totals * own_scale + other_totals * other_scale
    half_stat[...] = jnp.where(lane < 64, chip_top, chip_totals).reshape(NX, 32, 128)
    for k in (2, 1, 3):
        to = lax.rem(y + k + NX - x, NX)
        send(half_stat.at[to], far_stat.at[k - 1], bs_send.at[k - 1], bs_recv.at[k - 1], y_peer(k))
    for q, (at, size) in enumerate(PARTS):
        mine = jnp.dot(dispatch, tok[:, cols(q)], preferred_element_type=F32) * own_scale
        wait_for(sib_sums.at[:, :, cols(q)], a_recv.at[q])
        chip = mine + sib_sums[:, :, cols(q)].astype(F32).reshape(128, size) * other_scale
        own_sums[:, :, cols(q)] = chip.reshape(NX, 32, size)
        half[:, :, cols(q)] = chip.astype(BF).reshape(NX, 32, size)
        for k in (2, 1, 3):
            to = lax.rem(y + k + NX - x, NX)
            send(half.at[to, :, cols(q)], far.at[k - 1, :, cols(q)], b_send.at[q, k - 1], b_recv.at[q, k - 1], y_peer(k))

    key_rows = keys[...].reshape(256, D)
    for i in range(4):
        rows = slice(i * (tokens // 4), (i + 1) * (tokens // 4))
        logits = lax.dot_general(
            tok[rows, :], key_rows, (((1,), (1,)), ((), ())), preferred_element_type=F32
        )
        row_spread = jnp.exp(logits - jnp.max(logits, axis=1, keepdims=True))
        comb[rows, :] = (row_spread / jnp.sum(row_spread, axis=1, keepdims=True)).astype(BF)
    comb_out = pltpu.make_async_copy(comb, comb_ref, load_sem.at[7])
    comb_out.start()

    for k in (1, 3, 2):
        wait_for(far_stat.at[k - 1], bs_recv.at[k - 1])
    st = [half_stat[gx]] + [far_stat[k] for k in range(3)]
    ms = [s[:, 0:1] for s in st]
    ts = [s[:, 64:65] for s in st]
    m = jnp.maximum(jnp.maximum(ms[0], ms[1]), jnp.maximum(ms[2], ms[3]))
    fs = [jnp.exp(mi - m) for mi in ms]
    inv = 1.0 / (ts[0] * fs[0] + ts[1] * fs[1] + ts[2] * fs[2] + ts[3] * fs[3])
    fs = [f * inv for f in fs]

    def plane(src, there, s_sem, r_sem):
        for i in range(4):
            send_wide(src(i), there, s_sem.at[i], r_sem, (4 * h + i) * NX + gx)

    def gather_start(place, y_send, y_recv, s_send, s_recv):
        own = place(y, c)
        for k in (2, 1, 3):
            send(own, own, y_send.at[k - 1], y_recv.at[k - 1], y_peer(k))
        send(own, own, s_send.at[0], s_recv.at[0], sib)

    def gather_forward(place, y_send, y_recv, s_send, s_recv):
        for k in (1, 3, 2):
            got = place(lax.rem(y + NY - k, NY), c)
            wait_for(got, y_recv.at[k - 1])
            send(got, got, s_send.at[k], s_recv.at[k], sib)

    def gather_end(place, y_send, y_recv, s_send, s_recv):
        for k in range(NY):
            wait_for(place(lax.rem(y + NY - k, NY), 1 - c), s_recv.at[k])

    before = len(started)
    for q, (at, size) in enumerate(PARTS):
        for k in (1, 3, 2):
            wait_for(far.at[k - 1, :, cols(q)], b_recv.at[q, k - 1])
        acc = own_sums[gx, :, cols(q)] * fs[0]
        for k in range(3):
            acc = acc + far[k, :, cols(q)].astype(F32) * fs[k + 1]
        ready[:, :, cols(q)] = acc.reshape(4, OWN, size).astype(BF)
        plane(
            lambda i: ready.at[i, :, cols(q)], slots_in.at[y, c, lax.rem(z, 4), :, cols(q)], c_send.at[q], c_recv.at[q]
        )
    drain(before)

    def gather1(q):
        return (
            lambda yy, cc: slots_in.at[yy, cc, :, :, cols(q)], d_send.at[q], d_recv.at[q], e_send.at[q], e_recv.at[q]
        )

    for q in range(Q):
        wait_for(slots_in.at[y, c, :, :, cols(q)], c_recv.at[q])
        gather_start(*gather1(q))
    for q in range(Q):
        gather_forward(*gather1(q))

    for cp in loads[2:]:
        cp.wait()
    first = lax.rem(lax.broadcasted_iota(jnp.int32, (128, 1), 0), OWN) < 4
    bias = b_in[...].astype(F32)

    def hidden(core, arrive=lambda q: None):
        hid = None
        for q, (at, size) in enumerate(PARTS):
            arrive(q)
            rows_in = slots_in[:, core, :, :, cols(q)].reshape(128, size)
            term = jnp.dot(rows_in, win[cols(q), :], preferred_element_type=F32)
            hid = term if hid is None else hid + term
        hid = jnp.where(first, hid[:, :640] + bias[0:1], hid[:, 640:] + bias[1:2])
        hid = jax.nn.gelu(hid, approximate=True)
        return jnp.concatenate((jnp.where(first, hid, 0.0).astype(BF), jnp.where(first, 0.0, hid).astype(BF)), axis=1)

    hid_c = hidden(c)
    hid_sib = hidden(1 - c, lambda q: gather_end(*gather1(q)))
    for q, (at, size) in enumerate(PARTS):
        out = jnp.dot(hid_sib, wout[:, cols(q)], preferred_element_type=F32)
        part[:, :, cols(q)] = out.astype(BF).reshape(NY, 32, size)
        send(part.at[:, :, cols(q)], sib_part.at[:, :, cols(q)], f_send.at[q], f_recv.at[q], sib)
    for q, (at, size) in enumerate(PARTS):
        out = jnp.dot(hid_c, wout[:, cols(q)], preferred_element_type=F32)
        own_part[:, :, cols(q)] = out.reshape(NY, 32, size)

    before = len(started)
    for q, (at, size) in enumerate(PARTS):
        wait_for(sib_part.at[:, :, cols(q)], f_recv.at[q])
        chip = own_part[:, :, cols(q)] + sib_part[:, :, cols(q)].astype(F32)
        own_part[:, :, cols(q)] = chip
        half2[:, :, cols(q)] = chip.astype(BF)
        for k in (2, 1, 3):
            send(
                half2.at[lax.rem(y + k, NY), :, cols(q)], far2.at[k - 1, :, cols(q)],
                g_send.at[q, k - 1], g_recv.at[q, k - 1], y_peer(k),
            )
    drain(before)
    bias = b_out[...].astype(F32)
    first = lax.rem(lax.broadcasted_iota(jnp.int32, (32, 1), 0), OWN) < 4
    bias = jnp.where(first, bias[0:1], bias[1:2])
    before = len(started)
    for q, (at, size) in enumerate(PARTS):
        for k in (1, 3, 2):
            wait_for(far2.at[k - 1, :, cols(q)], g_recv.at[q, k - 1])
        acc = own_part[y, :, cols(q)] + bias[:, at:at + size]
        for k in range(3):
            acc = acc + far2[k, :, cols(q)].astype(F32)
        ready2[:, :, cols(q)] = acc.reshape(4, OWN, size).astype(BF)
        plane(
            lambda i: ready2.at[i, :, cols(q)], back.at[x, z // 4, lax.rem(z, 4), :, cols(q)], i_send.at[q], i_recv.at[q]
        )
    drain(before)

    def gather2(q):
        return (
            lambda yy, cc: back.at[lax.rem(yy + NX - x, NX), lax.rem(z // 4 + cc, 2), :, :, cols(q)],
            j_send.at[q], j_recv.at[q], k_send.at[q], k_recv.at[q],
        )

    for q in range(Q):
        wait_for(back.at[gx, h, :, :, cols(q)], i_recv.at[q])
        gather_start(*gather2(q))
    comb_out.wait()
    before = len(started)
    for q in range(Q):
        gather_forward(*gather2(q))
    drain(before)
    for q in range(Q):
        gather_end(*gather2(q))
    drain(len(started))


def mix(comb, slot_out, out_ref, out, sem):
    step = out.shape[0] // MIX_STEPS
    copies = []
    for i in range(MIX_STEPS):
        rows = pl.ds(i * step, step)
        out[rows, :] = jnp.dot(comb[rows, :], slot_out[...], preferred_element_type=F32).astype(BF)
        cp = pltpu.make_async_copy(out.at[rows], out_ref.at[rows], sem.at[i])
        cp.start()
        copies.append(cp)
    for cp in copies:
        cp.wait()


def on_device(tokens, slot_keys, w_in, b_in, w_out, b_out):
    rows = tokens.shape[1]
    slots = NZ * NX * OWN
    hbm = pl.BlockSpec(memory_space=pltpu.HBM)
    anywhere = pl.BlockSpec(memory_space=pl.ANY)
    dma = pltpu.SemaphoreType.DMA
    block = (4, OWN, D)
    comb, back = pl.pallas_call(
        kernel,
        out_shape=(
            pltpu.VMEM((rows, slots), BF),
            pltpu.VMEM((NX, 2) + block, BF),
        ),
        in_specs=[hbm] * 6,
        out_specs=(anywhere, anywhere),
        scratch_shapes=[
            pltpu.VMEM((rows, D), BF),
            pltpu.VMEM((D, rows), BF),
            pltpu.VMEM((D, D), BF),
            pltpu.VMEM((D, D), BF),
            pltpu.VMEM((2, 640), BF),
            pltpu.VMEM((2, D), BF),
            pltpu.VMEM((OWN, D), BF),
            pltpu.VMEM((NX, 2) + block, BF),
            pltpu.VMEM((slots // 2, rows), F32),
            pltpu.VMEM((rows, slots), BF),
            pltpu.VMEM((NX, 32, D), BF),
            pltpu.VMEM((NX, 32, 128), F32),
            pltpu.VMEM((NX, 32, D), BF),
            pltpu.VMEM((NX, 32, 128), F32),
            pltpu.VMEM((NX, 32, D), F32),
            pltpu.VMEM((NX, 32, D), BF),
            pltpu.VMEM((NX, 32, 128), F32),
            pltpu.VMEM((3, 32, D), BF),
            pltpu.VMEM((3, 32, 128), F32),
            pltpu.VMEM(block, BF),
            pltpu.VMEM((NY, 2) + block, BF),
            pltpu.VMEM((NY, 32, D), BF),
            pltpu.VMEM((NY, 32, D), F32),
            pltpu.VMEM((NY, 32, D), BF),
            pltpu.VMEM((NY, 32, D), BF),
            pltpu.VMEM((3, 32, D), BF),
            pltpu.VMEM(block, BF),
            dma((8,)), dma((16,)), dma((4,)), dma((4,)), dma((4,)),
            dma, dma, dma((Q,)), dma((Q,)), dma((3,)), dma((3,)), dma((Q, 3)), dma((Q, 3)),
            dma((Q, 4)), dma((Q,)), dma((Q, 3)), dma((Q, 3)), dma((Q, 4)), dma((Q, 4)),
            dma((Q,)), dma((Q,)), dma((Q, 3)), dma((Q, 3)),
            dma((Q, 4)), dma((Q,)), dma((Q, 3)), dma((Q, 3)), dma((Q, 4)), dma((Q, 4)),
        ],
        compiler_params=pltpu.CompilerParams(
            collective_id=0, has_side_effects=True, vmem_limit_bytes=48 * 1024 * 1024
        ),
    )(*(
        pltpu.with_memory_space_constraint(a, pltpu.HBM)
        for a in (tokens[0], slot_keys.T, w_in, b_in, w_out.reshape(-1, D), b_out)
    ))
    vmem = pl.BlockSpec(memory_space=pltpu.VMEM)
    return pl.pallas_call(
        mix,
        out_shape=jax.ShapeDtypeStruct((rows, D), BF),
        in_specs=[vmem, vmem],
        out_specs=anywhere,
        scratch_shapes=[pltpu.VMEM((rows, D), BF), dma((MIX_STEPS,))],
        compiler_params=pltpu.CompilerParams(vmem_limit_bytes=32 * 1024 * 1024),
    )(
        pltpu.with_memory_space_constraint(comb, pltpu.VMEM),
        pltpu.with_memory_space_constraint(back.reshape(slots, D), pltpu.VMEM),
    )[None]


def solution(mesh):
    in_specs = (
        P("wide", "narrow", None),
        P(None, "wide"),
        P("wide", None, "narrow"),
        P("wide", "narrow"),
        P("wide", "narrow", None),
        P("wide", None),
    )
    return jax.shard_map(
        on_device, mesh=mesh, in_specs=in_specs, out_specs=P("wide", "narrow", None), check_vma=False
    )
```
